32 devices in a mesh: row: 8 (over y, x, core), col: 4 (over z).
Axes of the slice: x: 2, y: 2, z: 4, core: 2. Of those that a mesh axis runs over, the one named last changes fastest.
Arguments:
- tokens: bfloat16 [128, 256, 512], P('row', 'col'), may hold values from -6 to 6
- grad_output: bfloat16 [128, 256, 512], P('row', 'col'), may hold values from -6 to 6
- w_exp: bfloat16 [512, 2048], replicated, may hold values from -0.375 to 0.375
- dw_kernel: float32 [3, 3, 2048], replicated, may hold values from -4.5 to 4.5
- w_proj: bfloat16 [2048, 512], replicated, may hold values from -0.125 to 0.125
- ln_gain: float32 [512], replicated, may hold values from 0.25 to 1.75
- w_qkv: bfloat16 [512, 1536], replicated, may hold values from -16 to 16
- w_out: bfloat16 [512, 512], replicated, may hold values from -0.25 to 0.25
Outputs:
- output: bfloat16 [128, 256, 512], P('row', 'col')
- grad_tokens: bfloat16 [128, 256, 512], P('row', 'col')
The draws below stay inside these ranges and needn't reach their ends.
All inputs are finite; a program needn't handle non-finite values.
Results may differ from the reference program's by a relative error of at most 0.03.
The reference program's roundings to bfloat16 on the way count: a program that leaves them out, or rounds other values in their place, can miss the bound.
Values may be sent and summed in bfloat16 or wider, within the bound.
A program may use at most 128 MiB of HBM per device.

```python
import jax
import jax.numpy as jnp
from jax import lax

C = 512
HEADS = 16
HD = 32
EXP = 2048
H = 128
W = 256


def draw_w_qkv(key, part):
    draw_base = jax.random.truncated_normal(key, -6.0, 6.0, (C, 3 * C), jnp.float32) * C ** (-0.5)
    return draw_base.astype(jnp.bfloat16)


def block_levels(key, shape, split, least, top_value):
    gain = 1.0
    for dim, parts in split:
        steps = jax.random.uniform(jax.random.fold_in(jax.random.fold_in(key, 6), dim), (parts,), jnp.float32, least / len(split), top_value / len(split))
        gain = gain * jnp.repeat(jnp.exp(steps), shape[dim] // parts).reshape((-1,) + (1,) * (len(shape) - 1 - dim))
    return gain


def noise(stream_key, dims, scale, limit, split=(), kind=jnp.bfloat16):
    result = scale * jax.random.normal(stream_key, dims, jnp.float32)
    if split:
        result = result * block_levels(stream_key, dims, split, -0.22, 0.18)
    return jnp.clip(result, -limit, limit).astype(kind)


def setup_inputs(seed: int = 0) -> dict:
    splits = jax.random.split(jax.random.key(seed), 9)
    return {
        "tokens": noise(splits[0], (H, W, C), 1.0, 6.0, ((0, 8), (1, 4))),
        "grad_output": noise(splits[1], (H, W, C), 1.0, 6.0, ((0, 8), (1, 4))),
        "w_exp": noise(splits[2], (C, EXP), (C // 2) ** -0.5, 0.375),
        "dw_kernel": noise(splits[3], (3, 3, EXP), 1.5, 4.5, (), jnp.float32),
        "w_proj": noise(splits[4], (EXP, C), EXP ** -0.5, 0.125),
        "ln_gain": jnp.clip(1.0 + 0.15 * jax.random.normal(splits[5], (C,), jnp.float32), 0.25, 1.75),
        "w_qkv": draw_w_qkv(jax.random.fold_in(splits[8], 71), 0),
        "w_out": noise(splits[7], (C, C), C ** -0.5, 0.25),
    }


root_two_pi = 0.7978845608028654
cubic_term = 0.044715
epsilon = 1e-05
band_rows = 8

def gelu_tanh(value_in):
    return 0.5 * value_in * (1.0 + jnp.tanh(root_two_pi * (value_in + cubic_term * value_in * value_in * value_in)))

def gelu_slope(value_in):
    tangent = jnp.tanh(root_two_pi * (value_in + cubic_term * value_in * value_in * value_in))
    return 0.5 * (1.0 + tangent) + 0.5 * value_in * (1.0 - tangent * tangent) * root_two_pi * (1.0 + 3.0 * cubic_term * value_in * value_in)

def depthwise(padded, kernel, out_rows, out_cols):
    summed = jnp.zeros((out_rows, out_cols, padded.shape[2]), jnp.float32)
    for row_off in range(3):
        for col_off in range(3):
            summed = summed + padded[row_off:row_off + out_rows, col_off:col_off + out_cols].astype(jnp.float32) * kernel[row_off, col_off]
    return summed

def depthwise_back(padded, kernel, out_rows, out_cols):
    summed = jnp.zeros((out_rows, out_cols, padded.shape[2]), jnp.float32)
    for row_off in range(3):
        for col_off in range(3):
            summed = summed + padded[2 - row_off:2 - row_off + out_rows, 2 - col_off:2 - col_off + out_cols].astype(jnp.float32) * kernel[row_off, col_off]
    return summed

def rounded(array):
    return lax.optimization_barrier(array.astype(jnp.bfloat16)).astype(jnp.float32)

def attend(hidden_win, grad_win, ln_gain, w_qkv, w_out):
    windows, members, width = hidden_win.shape
    hidden_f = hidden_win.astype(jnp.float32)
    center = hidden_f - lax.optimization_barrier(jnp.mean(hidden_f, axis=-1, keepdims=True))
    inv_std = lax.rsqrt(lax.optimization_barrier(jnp.mean(center * center, axis=-1, keepdims=True)) + epsilon)
    unit_norm = center * inv_std
    normed = (unit_norm * ln_gain).astype(jnp.bfloat16)
    packed = jnp.dot(normed.reshape(-1, width), w_qkv, preferred_element_type=jnp.float32)
    packed = rounded(packed).reshape(windows, members, 3, HEADS, HD)
    queries = packed[:, :, 0]
    key_rows = packed[:, :, 1]
    value_rows = packed[:, :, 2]
    score_scale = HD ** (-0.5)
    scores = jnp.einsum('wqhd,wkhd->whqk', queries, key_rows) * score_scale
    row_max = lax.optimization_barrier(jnp.max(scores, axis=-1, keepdims=True))
    lifted = jnp.exp(scores - row_max)
    attn_prob = lifted / lax.optimization_barrier(jnp.sum(lifted, axis=-1, keepdims=True))
    prob_round = rounded(attn_prob)
    attended = jnp.einsum('whqk,wkhd->wqhd', prob_round, value_rows).astype(jnp.bfloat16)
    attn = jnp.dot(attended.reshape(-1, width), w_out, preferred_element_type=jnp.float32).astype(jnp.bfloat16)
    grad_att = jnp.dot(grad_win.reshape(-1, width), w_out.T, preferred_element_type=jnp.float32)
    grad_att = rounded(grad_att).reshape(windows, members, HEADS, HD)
    grad_prob = jnp.einsum('wqhd,wkhd->whqk', grad_att, value_rows)
    grad_val = jnp.einsum('whqk,wqhd->wkhd', prob_round, grad_att).astype(jnp.bfloat16)
    grad_score = attn_prob * (grad_prob - lax.optimization_barrier(jnp.sum(grad_prob * attn_prob, axis=-1, keepdims=True))) * score_scale
    grad_score = rounded(grad_score)
    grad_query = jnp.einsum('whqk,wkhd->wqhd', grad_score, key_rows).astype(jnp.bfloat16)
    grad_key = jnp.einsum('whqk,wqhd->wkhd', grad_score, queries).astype(jnp.bfloat16)
    grad_pack = jnp.stack([grad_query, grad_key, grad_val], axis=2).reshape(-1, 3 * width)
    grad_norm = jnp.dot(grad_pack, w_qkv.T, preferred_element_type=jnp.float32)
    scaled = grad_norm.reshape(windows, members, width) * ln_gain
    grad_attn = inv_std * (scaled - lax.optimization_barrier(jnp.mean(scaled, axis=-1, keepdims=True)) - unit_norm * lax.optimization_barrier(jnp.mean(scaled * unit_norm, axis=-1, keepdims=True)))
    return (attn.reshape(windows, members, width), grad_attn.astype(jnp.bfloat16))

def reference(tokens, grad_output, w_exp, dw_kernel, w_proj, ln_gain, w_qkv, w_out):
    height, breadth, width = tokens.shape
    expand = w_exp.shape[1]
    tok_pad = jnp.pad(tokens, ((2, 2), (2, 2), (0, 0)))
    starts = jnp.arange(height // band_rows, dtype=jnp.int32) * band_rows

    def expand_band(start):
        row_block = lax.dynamic_slice_in_dim(tok_pad, start, band_rows + 4, 0)
        pre_pad = jnp.dot(row_block.reshape(-1, width), w_exp, preferred_element_type=jnp.float32).reshape(band_rows + 4, breadth + 4, expand)
        return (row_block, pre_pad, gelu_tanh(pre_pad).astype(jnp.bfloat16))

    def forward_band(start):
        row_block, pre_pad, act_pad = expand_band(start)
        conv_out = depthwise(act_pad[1:-1, 1:-1], dw_kernel, band_rows, breadth)
        gelu_out = gelu_tanh(conv_out).astype(jnp.bfloat16)
        interior = row_block[2:-2, 2:-2].astype(jnp.float32)
        branch = jnp.dot(gelu_out.reshape(-1, expand), w_proj, preferred_element_type=jnp.float32).reshape(band_rows, breadth, width)
        return (interior + branch).astype(jnp.bfloat16)
    hidden = lax.map(forward_band, starts).reshape(height, breadth, width)

    def to_windows(array):
        return array.reshape(8, height // 8, 8, breadth // 8, width).transpose(1, 3, 0, 2, 4).reshape(height // 8, breadth // 8, 64, width)

    def from_windows(array):
        return array.reshape(height // 8, breadth // 8, 8, 8, width).transpose(2, 0, 3, 1, 4).reshape(height, breadth, width)

    def window_row(window_pair):
        return attend(window_pair[0], window_pair[1], ln_gain, w_qkv, w_out)
    attn_win, grad_win = lax.map(window_row, (to_windows(hidden), to_windows(grad_output)))
    attn = from_windows(attn_win)
    grad_attn = from_windows(grad_win)
    output = (hidden.astype(jnp.float32) + attn.astype(jnp.float32)).astype(jnp.bfloat16)
    grad_hidden = grad_output.astype(jnp.float32) + grad_attn.astype(jnp.float32)
    grad_round = grad_hidden.astype(jnp.bfloat16)
    round_pad = jnp.pad(grad_round, ((1, 1), (1, 1), (0, 0)))

    def backward_band(start):
        row_block, pre_pad, act_pad = expand_band(start)
        conv_rim = depthwise(act_pad, dw_kernel, band_rows + 2, breadth + 2)
        grad_block = lax.dynamic_slice_in_dim(round_pad, start, band_rows + 2, 0)
        grad_mix = jnp.dot(grad_block.reshape(-1, width), w_proj.T, preferred_element_type=jnp.float32).reshape(band_rows + 2, breadth + 2, expand)
        grad_mid = (grad_mix * gelu_slope(conv_rim)).astype(jnp.bfloat16)
        grad_act = depthwise_back(grad_mid, dw_kernel, band_rows, breadth)
        grad_pre = (grad_act * gelu_slope(pre_pad[2:-2, 2:-2])).astype(jnp.bfloat16)
        residual = lax.dynamic_slice_in_dim(grad_hidden, start, band_rows, 0)
        branch = jnp.dot(grad_pre.reshape(-1, expand), w_exp.T, preferred_element_type=jnp.float32).reshape(band_rows, breadth, width)
        return (residual + branch).astype(jnp.bfloat16)
    grad_tokens = lax.map(backward_band, starts).reshape(height, breadth, width)
    return (output, grad_tokens)
```

```python
import functools

import jax
import jax.numpy as jnp
from jax import lax
from jax.experimental import pallas as pl
from jax.experimental.pallas import tpu as pltpu
from jax.sharding import PartitionSpec as P

HEADS = 16
HD = 32


root_two_pi = 0.7978845608028654
cubic_term = 0.044715
epsilon = 1e-05


def halo_of(cells, pad):
    rows, cols, width = cells.shape

    def exchange(head, tail, axis):
        count = lax.axis_size(axis)
        ends = count - 1
        before = lax.ppermute(tail, axis, [(i, i + 1) for i in range(ends)])
        after = lax.ppermute(head, axis, [(i + 1, i) for i in range(ends)])
        return before, after

    top, bottom = exchange(cells[:1], cells[-1:], "row")

    def column(index):
        parts = [top[:, index], cells[:, index], bottom[:, index]]
        return jnp.concatenate(parts, axis=0)

    left, right = exchange(column(0), column(cols - 1), "col")
    fill = jnp.zeros((pad - rows - 2, width), cells.dtype)
    return jnp.concatenate([top[0], bottom[0], left, fill, right, fill], axis=0)


def gelu_and_slope(value_in):
    square = value_in * value_in
    tangent = jnp.tanh(value_in * (root_two_pi + root_two_pi * cubic_term * square))
    half = 0.5 * tangent + 0.5
    gelu = value_in * half
    slope = half + gelu * (1.0 - half) * (2.0 * root_two_pi + 6.0 * root_two_pi * cubic_term * square)
    return gelu, slope


def place_halo(block, padded, sides, rows, cols):
    padded[0:cols, :] = block[0:cols]
    padded[(rows + 1) * cols : (rows + 2) * cols, :] = block[cols : 2 * cols]
    sides[...] = block[2 * cols :].astype(jnp.float32)


def depthwise_rows(rows, cols, pad, padded, sides, taps, finish):
    place = lax.broadcasted_iota(jnp.int32, (cols, 128), 0)

    for index in range(rows):
        for start in range(0, padded.shape[1], 128):
            lanes = pl.ds(start, 128)
            near = [
                padded[pl.ds((index + a) * cols, cols), lanes].astype(
                    jnp.float32
                )
                for a in range(3)
            ]

            def tap(a, b):
                return taps[3 * a + b : 3 * a + b + 1, lanes]

            def column(b):
                return near[0] * tap(0, b) + near[1] * tap(1, b) + near[2] * tap(2, b)

            def side(first, b):
                return (
                    sides[pl.ds(first + index, 1), lanes] * tap(0, b)
                    + sides[pl.ds(first + index + 1, 1), lanes] * tap(1, b)
                    + sides[pl.ds(first + index + 2, 1), lanes] * tap(2, b)
                )

            before = jnp.where(place == 0, side(0, 0), pltpu.roll(column(0), 1, 0))
            after = jnp.where(place == cols - 1, side(pad, 2), pltpu.roll(column(2), cols - 1, 0))
            finish(
                pl.ds(index * cols, cols), lanes, before + column(1) + after
            )


def chunks_of(total):
    size = 256 if total % 256 == 0 else total
    return [(start, size) for start in range(0, total, size)]


def forward_kernel(
    rows, cols, pad, x_ref, halo_ref, w_exp_ref, taps, w_proj_ref, hidden_ref, slope_pre_ref,
    slope_conv_ref, padded, sides, gelu_out, total,
):
    f32, bf16 = jnp.float32, jnp.bfloat16
    step = pl.program_id(0)
    w_exp = w_exp_ref[...]
    edge = jnp.dot(halo_ref[...], w_exp, preferred_element_type=f32)
    place_halo(gelu_and_slope(edge)[0].astype(bf16), padded, sides, rows, cols)
    for start, size in chunks_of(rows * cols):
        pre_act = jnp.dot(x_ref[start : start + size, :], w_exp, preferred_element_type=f32)
        gelu, slope = gelu_and_slope(pre_act)
        padded[cols + start : cols + start + size, :] = gelu.astype(bf16)
        slope_pre_ref[start : start + size, :] = slope.astype(bf16)

    def finish(where, lanes, conv_out):
        gelu, slope = gelu_and_slope(conv_out)
        gelu_out[where, lanes] = gelu.astype(bf16)
        slope_conv_ref[where, lanes] = slope.astype(bf16)

    depthwise_rows(rows, cols, pad, padded, sides, taps, finish)

    @pl.when(step == 0)
    def _():
        total[...] = x_ref[...].astype(f32)

    for start, size in chunks_of(rows * cols):
        total[start : start + size, :] += jnp.dot(
            gelu_out[start : start + size, :], w_proj_ref[...], preferred_element_type=f32
        )

    @pl.when(step == pl.num_programs(0) - 1)
    def _():
        hidden_ref[...] = total[...].astype(bf16)


def backward_kernel(
    rows, cols, pad, gout_ref, gattn_ref, halo_ref, w_proj_ref, slope_conv_ref, slope_halo_ref, taps,
    slope_pre_ref, w_exp_ref, gtok_ref, padded, sides, grad_pre, total, rounded,
):
    f32, bf16 = jnp.float32, jnp.bfloat16
    nt = (((1,), (1,)), ((), ()))
    step = pl.program_id(0)

    @pl.when(step == 0)
    def _():
        grad_hidden = gout_ref[...].astype(f32) + gattn_ref[...].astype(f32)
        total[...] = grad_hidden
        rounded[...] = grad_hidden.astype(bf16)

    w_proj = w_proj_ref[...]
    edge = lax.dot_general(halo_ref[...], w_proj, nt, preferred_element_type=f32)
    place_halo((edge * slope_halo_ref[...].astype(f32)).astype(bf16), padded, sides, rows, cols)
    for start, size in chunks_of(rows * cols):
        grad_mix = lax.dot_general(
            rounded[start : start + size, :], w_proj, nt, preferred_element_type=f32
        )
        padded[cols + start : cols + start + size, :] = (
            grad_mix * slope_conv_ref[start : start + size, :].astype(f32)
        ).astype(bf16)

    def finish(where, lanes, grad_act):
        grad_pre[where, lanes] = (grad_act * slope_pre_ref[where, lanes].astype(f32)).astype(bf16)

    depthwise_rows(rows, cols, pad, padded, sides, taps, finish)
    for start, size in chunks_of(rows * cols):
        total[start : start + size, :] += lax.dot_general(
            grad_pre[start : start + size, :], w_exp_ref[...], nt, preferred_element_type=f32
        )

    @pl.when(step == pl.num_programs(0) - 1)
    def _():
        gtok_ref[...] = total[...].astype(bf16)


def mbconv_call(kernel, rows, cols, pad, operands, kinds, out_kinds, extra, width, expand):
    cells = rows * cols
    edge = 2 * cols + 2 * pad
    block = 256
    specs = {
        "cells": pl.BlockSpec((cells, width), lambda i: (0, 0)),
        "edge": pl.BlockSpec((edge, width), lambda i: (0, 0)),
        "exp": pl.BlockSpec((width, block), lambda i: (0, i)),
        "taps": pl.BlockSpec((9, block), lambda i: (0, i)),
        "proj": pl.BlockSpec((block, width), lambda i: (i, 0)),
        "wide": pl.BlockSpec((cells, block), lambda i: (0, i)),
        "wide_edge": pl.BlockSpec((edge, block), lambda i: (0, i)),
    }
    shapes = {"cells": (cells, width), "wide": (cells, expand)}
    return pl.pallas_call(
        functools.partial(kernel, rows, cols, pad),
        grid=(expand // block,),
        in_specs=[specs[kind] for kind in kinds],
        out_specs=[specs[kind] for kind in out_kinds],
        out_shape=[jax.ShapeDtypeStruct(shapes[kind], jnp.bfloat16) for kind in out_kinds],
        scratch_shapes=[
            pltpu.VMEM(((rows + 2) * cols, block), jnp.bfloat16),
            pltpu.VMEM((2 * pad, block), jnp.float32),
            pltpu.VMEM((cells, block), jnp.bfloat16),
            pltpu.VMEM((cells, width), jnp.float32),
        ]
        + extra,
        compiler_params=pltpu.CompilerParams(vmem_limit_bytes=40 * 1024 * 1024),
        cost_estimate=pl.CostEstimate(
            flops=40 * cells * width * expand // 4, bytes_accessed=4 * cells * expand, transcendentals=0
        ),
    )(*operands)


def attend_kernel(
    hidden_ref, grad_ref, gain_ref, w_qkv_ref, w_out_ref, attn_ref, gattn_ref, pack, gatt, att, gpack
):
    width = hidden_ref.shape[1]
    f32, bf16 = jnp.float32, jnp.bfloat16
    nt = (((1,), (1,)), ((), ()))
    tn = (((0,), (0,)), ((), ()))
    hidden_f = hidden_ref[...].astype(f32)
    center = hidden_f - jnp.mean(hidden_f, axis=-1, keepdims=True)
    inv_std = lax.rsqrt(jnp.mean(center * center, axis=-1, keepdims=True) + epsilon)
    unit_norm = center * inv_std
    gain = gain_ref[...]
    normed = (unit_norm * gain).astype(bf16)
    pack[...] = jnp.dot(normed, w_qkv_ref[...], preferred_element_type=f32).astype(bf16)
    gatt[...] = lax.dot_general(
        grad_ref[...], w_out_ref[...], nt, preferred_element_type=f32
    ).astype(bf16)
    per = 128 // HD
    head_row = lax.broadcasted_iota(jnp.int32, (per * 64, 128), 0) // 64
    head_lane = lax.broadcasted_iota(jnp.int32, (per * 64, 128), 1) // HD
    same = head_row == head_lane
    score_scale = HD ** (-0.5)

    def spread(block):
        return jnp.where(same, jnp.concatenate([block] * per, axis=0), jnp.zeros((), bf16))

    def gather(block):
        kept = jnp.where(same, block, 0.0)
        total = kept[0:64]
        for h in range(1, per):
            total = total + kept[h * 64 : (h + 1) * 64]
        return total.astype(bf16)

    def window(index, carry):
        rows = pl.ds(pl.multiple_of(index * 64, 64), 64)
        for start in range(0, width, 128):
            lanes = pl.ds(start, 128)
            lanes_k = pl.ds(width + start, 128)
            lanes_v = pl.ds(2 * width + start, 128)
            queries, key_rows, values = pack[rows, lanes], pack[rows, lanes_k], pack[rows, lanes_v]
            query_bd = spread(queries)
            grad_bd = spread(gatt[rows, lanes])
            scores = lax.dot_general(key_rows, query_bd, nt, preferred_element_type=f32) * score_scale
            lifted = jnp.exp(scores - jnp.max(scores, axis=0, keepdims=True))
            prob = lifted * (1.0 / jnp.sum(lifted, axis=0, keepdims=True))
            prob_round = prob.astype(bf16)
            grad_prob = lax.dot_general(values, grad_bd, nt, preferred_element_type=f32)
            inner = jnp.sum(grad_prob * prob, axis=0, keepdims=True)
            grad_score = (prob * (grad_prob - inner) * score_scale).astype(bf16)
            att[rows, lanes] = gather(
                lax.dot_general(prob_round, values, tn, preferred_element_type=f32)
            )
            gpack[rows, lanes] = gather(
                lax.dot_general(grad_score, key_rows, tn, preferred_element_type=f32)
            )
            gpack[rows, lanes_k] = jnp.dot(
                grad_score, query_bd, preferred_element_type=f32
            ).astype(bf16)
            gpack[rows, lanes_v] = jnp.dot(
                prob_round, grad_bd, preferred_element_type=f32
            ).astype(bf16)
        return carry

    lax.fori_loop(0, hidden_ref.shape[0] // 64, window, 0)
    attn_ref[...] = jnp.dot(att[...], w_out_ref[...], preferred_element_type=f32).astype(bf16)
    grad_norm = lax.dot_general(gpack[...], w_qkv_ref[...], nt, preferred_element_type=f32)
    scaled = grad_norm * gain
    gattn_ref[...] = (
        inv_std
        * (
            scaled
            - jnp.mean(scaled, axis=-1, keepdims=True)
            - unit_norm * jnp.mean(scaled * unit_norm, axis=-1, keepdims=True)
        )
    ).astype(bf16)


def attend(hidden_win, grad_win, ln_gain, w_qkv, w_out):
    windows, members, width = hidden_win.shape
    rows = windows * members
    block = 256 if rows % 256 == 0 else 64
    tokens_spec = pl.BlockSpec((block, width), lambda i: (i, 0))

    def whole(shape):
        return pl.BlockSpec(shape, lambda i: (0, 0))

    attn, gattn = pl.pallas_call(
        attend_kernel,
        grid=(rows // block,),
        in_specs=[
            tokens_spec,
            tokens_spec,
            whole((1, width)),
            whole(w_qkv.shape),
            whole(w_out.shape),
        ],
        out_specs=[tokens_spec, tokens_spec],
        out_shape=[jax.ShapeDtypeStruct((rows, width), jnp.bfloat16)] * 2,
        scratch_shapes=[
            pltpu.VMEM((block, 3 * width), jnp.bfloat16),
            pltpu.VMEM((block, width), jnp.bfloat16),
            pltpu.VMEM((block, width), jnp.bfloat16),
            pltpu.VMEM((block, 3 * width), jnp.bfloat16),
        ],
        compiler_params=pltpu.CompilerParams(vmem_limit_bytes=40 * 1024 * 1024),
        cost_estimate=pl.CostEstimate(
            flops=24 * rows * width * width, bytes_accessed=8 * rows * width, transcendentals=0
        ),
    )(
        hidden_win.reshape(rows, width),
        grad_win.reshape(rows, width),
        ln_gain.reshape(1, width),
        w_qkv,
        w_out,
    )
    return attn.reshape(windows, members, width), gattn.reshape(windows, members, width)


def tile_windows(array, tile_rows, tile_cols):
    width = array.shape[-1]
    five_way = array.reshape(8, tile_rows // 8, 8, tile_cols // 8, width).transpose(1, 3, 0, 2, 4)
    return five_way.reshape(tile_rows // 8 * (tile_cols // 8), 64, width)


def untile_windows(array, tile_rows, tile_cols):
    width = array.shape[-1]
    five_way = array.reshape(tile_rows // 8, tile_cols // 8, 8, 8, width).transpose(2, 0, 3, 1, 4)
    return five_way.reshape(tile_rows, tile_cols, width)


def per_device(tokens, grad_output, w_exp, dw_kernel, w_proj, ln_gain, w_qkv, w_out):
    tile_rows, tile_cols, width = tokens.shape
    expand = w_exp.shape[1]
    row_count = lax.axis_size("row")
    col_count = lax.axis_size("col")
    row_step = tile_rows // row_count
    col_step = tile_cols // col_count
    cells = tile_rows * tile_cols
    pad = (tile_rows + 2 + 15) // 16 * 16
    taps = dw_kernel.reshape(9, expand)
    hidden, slope_pre, slope_conv = mbconv_call(
        forward_kernel,
        tile_rows,
        tile_cols,
        pad,
        (tokens.reshape(cells, width), halo_of(tokens, pad), w_exp, taps, w_proj),
        ("cells", "edge", "exp", "taps", "proj"),
        ("cells", "wide", "wide"),
        [],
        width,
        expand,
    )
    slope_halo = halo_of(slope_conv.reshape(tile_rows, tile_cols, expand), pad)
    hidden = hidden.reshape(tile_rows, tile_cols, width)

    def peer_major(array):
        five_way = array.reshape(row_step, row_count, col_step, col_count, width).transpose(
            1, 3, 0, 2, 4
        )
        return five_way.reshape(row_count * col_count, row_step, col_step, width)

    def source_major(array):
        five_way = array.reshape(row_count, col_count, row_step, col_step, width).transpose(
            0, 2, 1, 3, 4
        )
        return five_way.reshape(tile_rows, tile_cols, width)

    received = (
        lax.all_to_all(peer_major(hidden), ("row", "col"), split_axis=0, concat_axis=0, tiled=True),
        lax.all_to_all(
            peer_major(grad_output), ("row", "col"), split_axis=0, concat_axis=0, tiled=True
        ),
    )
    hidden_grid = source_major(received[0])
    grad_grid = source_major(received[1])
    attn_win, grad_win = attend(
        tile_windows(hidden_grid, tile_rows, tile_cols),
        tile_windows(grad_grid, tile_rows, tile_cols),
        ln_gain,
        w_qkv,
        w_out,
    )
    attn_grid = untile_windows(attn_win, tile_rows, tile_cols)
    grad_attn_grid = untile_windows(grad_win, tile_rows, tile_cols)

    def owner_major(array):
        five_way = array.reshape(row_count, row_step, col_count, col_step, width).transpose(
            0, 2, 1, 3, 4
        )
        return five_way.reshape(row_count * col_count, row_step, col_step, width)

    def back_to_tile(array):
        five_way = array.reshape(row_count, col_count, row_step, col_step, width).transpose(
            2, 0, 3, 1, 4
        )
        return five_way.reshape(tile_rows, tile_cols, width)

    returned = (
        lax.all_to_all(
            owner_major(attn_grid), ("row", "col"), split_axis=0, concat_axis=0, tiled=True
        ),
        lax.all_to_all(
            owner_major(grad_attn_grid), ("row", "col"), split_axis=0, concat_axis=0, tiled=True
        ),
    )
    attn = back_to_tile(returned[0])
    grad_attn = back_to_tile(returned[1])
    output = (hidden.astype(jnp.float32) + attn.astype(jnp.float32)).astype(jnp.bfloat16)
    grad_round = (grad_output.astype(jnp.float32) + grad_attn.astype(jnp.float32)).astype(
        jnp.bfloat16
    )
    grad_tokens = mbconv_call(
        backward_kernel,
        tile_rows,
        tile_cols,
        pad,
        (
            grad_output.reshape(cells, width),
            grad_attn.reshape(cells, width),
            halo_of(grad_round, pad),
            w_proj,
            slope_conv,
            slope_halo,
            taps[::-1],
            slope_pre,
            w_exp,
        ),
        ("cells", "cells", "edge", "proj", "wide", "wide_edge", "taps", "wide", "exp"),
        ("cells",),
        [pltpu.VMEM((cells, width), jnp.bfloat16)],
        width,
        expand,
    )[0]
    return (output, grad_tokens.reshape(tile_rows, tile_cols, width))


def solution(mesh):
    in_specs = (P("row", "col", None), P("row", "col", None), P(), P(), P(), P(), P(), P())
    out_specs = (P("row", "col", None), P("row", "col", None))
    return jax.shard_map(
        per_device, mesh=mesh, in_specs=in_specs, out_specs=out_specs, check_vma=False
    )
```
